32 devices in a mesh: dp: 4 (over z), ctx: 4 (over y, x), head: 2 (over core).
Axes of the slice: x: 2, y: 2, z: 4, core: 2. Of those that a mesh axis runs over, the one named last changes fastest.
Arguments:
- queries: bfloat16 [4, 1024, 12, 128], P('dp', 'ctx', 'head'), may hold values from -6 to 6
- keys: bfloat16 [4, 1024, 12, 128], P('dp', 'ctx', 'head'), may hold values from -0.5 to 0.5
- values: bfloat16 [4, 1024, 12, 128], P('dp', 'ctx', 'head'), may hold values from -6 to 6
- hidden_in: bfloat16 [4, 1024, 3072], P('dp', 'ctx'), may hold values from -6 to 6
- rate_weight: bfloat16 [12, 3072], P('head'), may hold values from -0.109375 to 0.109375
- state_init: float32 [12, 128, 128], P('head'), may hold values from -0.5 to 0.5
- out_grad: bfloat16 [4, 1024, 12, 128], P('dp', 'ctx', 'head'), may hold values from -6 to 6
Outputs:
- grad_queries: bfloat16 [4, 1024, 12, 128], P('dp', 'ctx', 'head')
- grad_keys: bfloat16 [4, 1024, 12, 128], P('dp', 'ctx', 'head')
- grad_values: bfloat16 [4, 1024, 12, 128], P('dp', 'ctx', 'head')
- grad_hidden: bfloat16 [4, 1024, 3072], P('dp', 'ctx')
- grad_rate_weight: float32 [12, 3072], P('head')
- grad_init: float32 [12, 128, 128], P('head')
The draws below stay inside these ranges and needn't reach their ends.
All inputs are finite; a program needn't handle non-finite values.
Results may differ from the reference program's by a relative error of at most 0.0051.
Values may be sent and summed in bfloat16 or wider, within the bound.
A program may use at most 192 MiB of HBM per device.

```python
import jax
import jax.numpy as jnp
from jax import lax

D = 3072
HEAD = 128
HEADS = 12
MINI = 64
SEQS = 4
LENGTH = 1024
N_HEAD = 2


def shard_levels(own_key, dims, split, low, high):
    level = 1.0
    for dim, shards_of in split:
        steps = jax.random.uniform(jax.random.fold_in(jax.random.fold_in(own_key, 6), dim), (shards_of,), jnp.float32, low / len(split), high / len(split))
        level = level * jnp.repeat(jnp.exp(steps), dims[dim] // shards_of).reshape((-1,) + (1,) * (len(dims) - 1 - dim))
    return level


def noise(own_key, extent, deviation, limit, cuts=(), dtype=jnp.bfloat16):
    entries = deviation * jax.random.normal(own_key, extent, jnp.float32)
    if cuts:
        entries = entries * shard_levels(own_key, extent, cuts, -0.22, 0.18)
    return jnp.clip(entries, -limit, limit).astype(dtype)


def setup_inputs(seed: int = 0) -> dict:
    seeds = jax.random.split(jax.random.key(seed), 8)
    queries = noise(seeds[0], (SEQS, LENGTH, HEADS, HEAD), 1.0, 6.0, ((0, 4), (1, 4), (2, 2)))
    keys = noise(seeds[1], (SEQS, LENGTH, HEADS, HEAD), 0.09, 0.5, ((0, 4), (1, 4), (2, 2)))
    values = noise(seeds[2], (SEQS, LENGTH, HEADS, HEAD), 1.0, 6.0, ((0, 4), (1, 4), (2, 2)))
    hidden_in = noise(seeds[3], (SEQS, LENGTH, D), 1.0, 6.0, ((0, 4), (1, 4)))
    rate_weight = noise(seeds[4], (HEADS, D), D ** -0.5, 0.109375, ((0, 2),))
    state_init = noise(seeds[5], (HEADS, HEAD, HEAD), HEAD ** -0.5, 0.5, ((0, 2),), jnp.float32)
    out_grad = noise(seeds[6], (SEQS, LENGTH, HEADS, HEAD), 1.0, 6.0, ((0, 4), (1, 4), (2, 2)))
    return {"queries": queries, "keys": keys, "values": values, "hidden_in": hidden_in, "rate_weight": rate_weight, "state_init": state_init, "out_grad": out_grad}


RATE_SCALE = 0.5

def product(left, right):
    return jnp.dot(left, right, precision=lax.Precision.HIGHEST, preferred_element_type=jnp.float32)

def local_run(state, query_rows, key_rows, value_rows, logit_rows):
    rates = RATE_SCALE * jax.nn.sigmoid(logit_rows)
    block_count = query_rows.shape[0] // MINI
    width = query_rows.shape[1]

    def advance(current, block):
        query_block, key_block, value_block, rate_block = block
        residual = product(key_block, current) - value_block
        current = current - product(key_block.T, rate_block[:, None] * residual)
        return (current, product(query_block, current))
    blocks = (query_rows.reshape(block_count, MINI, width), key_rows.reshape(block_count, MINI, width), value_rows.reshape(block_count, MINI, width), rates.reshape(block_count, MINI))
    final_state, layer_rows = lax.scan(advance, state, blocks)
    return (final_state, layer_rows.reshape(query_rows.shape))

def arrange(array):
    return jnp.transpose(array.astype(jnp.float32), (0, 2, 1, 3))

def reference(queries, keys, values, hidden_in, rate_weight, state_init, out_grad):
    logits = jnp.dot(hidden_in.reshape(SEQS * LENGTH, D), rate_weight.T, preferred_element_type=jnp.float32)
    logit_rows = jnp.transpose(logits.reshape(SEQS, LENGTH, HEADS), (0, 2, 1))

    def whole(query_all, key_all, value_all, logit_all, init_all):

        def one_head(state, query_rows, key_rows, value_rows, rows_logit):
            return local_run(state, query_rows, key_rows, value_rows, rows_logit)[1]
        per_seq = jax.vmap(one_head, in_axes=(0, 0, 0, 0, 0))
        return jax.vmap(per_seq, in_axes=(None, 0, 0, 0, 0))(init_all, query_all, key_all, value_all, logit_all)
    layer_out, pullback = jax.vjp(whole, arrange(queries), arrange(keys), arrange(values), logit_rows, state_init)
    grad_query, grad_key, grad_value, grad_logit, grad_init = pullback(arrange(out_grad))
    logit_flat = jnp.transpose(grad_logit, (0, 2, 1)).reshape(SEQS * LENGTH, HEADS)
    inputs_flat = hidden_in.reshape(SEQS * LENGTH, D)
    grad_rate_weight = jnp.dot(logit_flat.T, inputs_flat.astype(jnp.float32), precision=lax.Precision.HIGHEST, preferred_element_type=jnp.float32)
    group_width = HEADS // N_HEAD
    weight_float = rate_weight.astype(jnp.float32)
    total = jnp.zeros((SEQS * LENGTH, D), jnp.float32)
    for group in range(N_HEAD):
        term = product(logit_flat[:, group * group_width:(group + 1) * group_width], weight_float[group * group_width:(group + 1) * group_width]).astype(jnp.bfloat16)
        term = lax.optimization_barrier(term)
        total = total + term.astype(jnp.float32)
    grad_hidden = total.astype(jnp.bfloat16).reshape(SEQS, LENGTH, D)

    def back(array):
        return jnp.transpose(array, (0, 2, 1, 3)).astype(jnp.bfloat16)
    return (back(grad_query), back(grad_key), back(grad_value), grad_hidden, grad_rate_weight, grad_init)
```

```python
import functools

import jax
import jax.numpy as jnp
from jax import lax
from jax.experimental import pallas as pl
from jax.experimental.pallas import tpu as pltpu
from jax.sharding import PartitionSpec as P

MINI = 64
RATE_SCALE = 0.5
F32 = jnp.float32
BF16 = jnp.bfloat16
MESH = pl.DeviceIdType.MESH
SPAN = 256


def dot_nn(left, right):
    return jnp.dot(left, right, preferred_element_type=F32)


def dot_tn(left, right):
    return lax.dot_general(left, right, (((0,), (0,)), ((), ())), preferred_element_type=F32)


def dot_nt(left, right):
    return lax.dot_general(left, right, (((1,), (1,)), ((), ())), preferred_element_type=F32)


def b16(value):
    return value.astype(BF16)


def split(value):
    high = b16(value)
    return high, b16(value - high.astype(F32))


def kernel(
    n_dp, n_ctx, n_red, heads, width, toks,
    q_ref, k_ref, v_ref, hid_ref, rw_ref, init_ref, o_ref,
    dq_ref, dk_ref, dv_ref, gh_ref, gw_ref, gi_ref,
    own, lev_send, lev_recv, top_send, top_recv, qo, run_x, run_p, run_res,
    rw_other, dl_send, dl_recv, gi_send, gi_recv, gi_red, gi_all,
    gw_part, gw_recv, gw_red, gw_all,
    lev_ss, lev_rs, top_ss, top_rs, rw_sem, dl_sem,
    gi_ss, gi_rs, gi_as, gi_ar, gw_ss, gw_rs, gw_as, gw_ar,
):
    dp, ctx, head = lax.axis_index("dp"), lax.axis_index("ctx"), lax.axis_index("head")
    levels = n_ctx.bit_length() - 1
    red_ctx = n_red // n_dp
    n_src = n_dp * n_ctx
    me = dp * n_ctx + ctx
    my_red = dp * red_ctx + ctx
    is_red = ctx < red_ctx
    blocks = toks // MINI
    piece_rows = heads * width // n_red
    other_head = {"head": 1 - head}

    barrier = pltpu.get_barrier_semaphore()

    def greet(step, carry):
        peer = lax.rem(me + step, n_src)
        pl.semaphore_signal(
            barrier, inc=1,
            device_id={"dp": peer // n_ctx, "ctx": lax.rem(peer, n_ctx)},
            device_id_type=MESH,
        )
        return carry

    lax.fori_loop(1, n_src, greet, 0)
    pl.semaphore_signal(barrier, inc=1, device_id=other_head, device_id_type=MESH)

    logits = dot_nt(hid_ref[...], rw_ref[...])
    sig = 1.0 / (1.0 + jnp.exp(-logits))
    rates = RATE_SCALE * sig
    slope = RATE_SCALE * sig * (1.0 - sig)
    eye = (
        lax.broadcasted_iota(jnp.int32, (width, width), 0)
        == lax.broadcasted_iota(jnp.int32, (width, width), 1)
    ).astype(F32)
    start = jnp.concatenate([eye, jnp.zeros((width, width), F32)], axis=1)

    def rows(b):
        return slice(b * MINI, (b + 1) * MINI)

    def lanes(h):
        return slice(h * width, (h + 1) * width)

    def rate(b, h):
        return rates[b * MINI : (b + 1) * MINI, h : h + 1]

    def level_copy(level, h):
        partner = jnp.bitwise_xor(ctx, 1 << level)
        return pltpu.make_async_remote_copy(
            src_ref=lev_send.at[level, h], dst_ref=lev_recv.at[level, h],
            send_sem=lev_ss.at[level, h], recv_sem=lev_rs.at[level, h],
            device_id={"ctx": partner}, device_id_type=MESH,
        )

    def top_copy(h):
        partner = jnp.bitwise_xor(ctx, 1 << (levels - 1))
        return pltpu.make_async_remote_copy(
            src_ref=top_send.at[h], dst_ref=top_recv.at[h],
            send_sem=top_ss.at[h], recv_sem=top_rs.at[h],
            device_id={"ctx": partner}, device_id_type=MESH,
        )

    rw_copy = pltpu.make_async_remote_copy(
        src_ref=rw_ref, dst_ref=rw_other, send_sem=rw_sem.at[0], recv_sem=rw_sem.at[1],
        device_id=other_head, device_id_type=MESH,
    )
    dl_copy = pltpu.make_async_remote_copy(
        src_ref=dl_send, dst_ref=dl_recv, send_sem=dl_sem.at[0], recv_sem=dl_sem.at[1],
        device_id=other_head, device_id_type=MESH,
    )

    def local_maps(group):
        fwd = {h: start for h in group}
        back = {h: None for h in group}
        for step in range(blocks):
            b = step
            for h in group:
                key = k_ref[rows(b), lanes(h)]
                val = v_ref[rows(b), lanes(h)].astype(F32)
                if step == 0:
                    res = jnp.concatenate([key.astype(F32), -val], axis=1)
                else:
                    res = dot_nn(key, b16(fwd[h]))
                    res = jnp.concatenate([res[:, :width], res[:, width:] - val], axis=1)
                fwd[h] = fwd[h] - dot_tn(key, b16(rate(b, h) * res))
            b = blocks - 1 - step
            for h in group:
                key = k_ref[rows(b), lanes(h)]
                term = dot_tn(q_ref[rows(b), lanes(h)], o_ref[rows(b), lanes(h)])
                qo[h, b] = term
                total = term if step == 0 else back[h] + term
                back[h] = total - dot_tn(key, b16(rate(b, h) * dot_nn(key, b16(total))))
        for h in group:
            own[h, 0] = fwd[h][:, :width]
            own[h, 1] = fwd[h][:, width:]
            own[h, 2] = back[h]
            lev_send[0, h, 0] = b16(fwd[h][:, :width])
            lev_send[0, h, 1] = b16(fwd[h][:, width:])
            lev_send[0, h, 2] = b16(back[h])

    third = max(heads // 3, 1)
    groups = [list(range(i, min(i + third, heads))) for i in range(0, heads, third)]
    for index, group in enumerate(groups):
        local_maps(group)
        if index == 0:
            pl.semaphore_wait(barrier, n_src)
            rw_copy.start()
        for h in group:
            level_copy(0, h).start()

    prefix, suffix = {}, {}
    comp = {}
    for level in range(levels - 1):
        late = lax.rem(ctx // (1 << level), 2) == 1
        for h in range(heads):
            level_copy(level, h).wait_recv()
            map_in, shift_in, back_in = (lev_recv[level, h, i] for i in range(3))
            if level == 0:
                map_own, shift_own, back_own = (own[h, i] for i in range(3))
                prefix[h] = (
                    jnp.where(late, map_in.astype(F32), eye),
                    jnp.where(late, shift_in.astype(F32), 0.0),
                )
                suffix[h] = (
                    jnp.where(late, eye, map_in.astype(F32)),
                    jnp.where(late, 0.0, back_in.astype(F32)),
                )
            else:
                map_own, shift_own, back_own = comp[h]
                pre_map, pre_shift = prefix[h]
                suf_map, suf_shift = suffix[h]
                prefix[h] = (
                    jnp.where(late, dot_nn(b16(pre_map), map_in), pre_map),
                    jnp.where(late, dot_nn(b16(pre_map), shift_in) + pre_shift, pre_shift),
                )
                suffix[h] = (
                    jnp.where(late, suf_map, dot_nn(map_in, b16(suf_map))),
                    jnp.where(late, suf_shift, dot_tn(b16(suf_map), back_in) + suf_shift),
                )
            early_map = jnp.where(late, map_in, b16(map_own))
            late_map = jnp.where(late, b16(map_own), map_in)
            early_shift = jnp.where(late, shift_in, b16(shift_own))
            late_shift = jnp.where(late, shift_own, shift_in.astype(F32))
            early_back = jnp.where(late, back_in.astype(F32), back_own)
            late_back = jnp.where(late, b16(back_own), back_in)
            both = dot_nn(late_map, jnp.concatenate([early_map, early_shift], axis=1))
            comp[h] = (
                both[:, :width],
                both[:, width:] + late_shift,
                dot_tn(early_map, late_back) + early_back,
            )
            if level < levels - 2:
                for i in range(3):
                    lev_send[level + 1, h, i] = b16(comp[h][i])
                level_copy(level + 1, h).start()
            else:
                upper = ctx // (1 << (levels - 1)) == 1
                middle = dot_nn(b16(comp[h][0]), b16(init_ref[h])) + comp[h][1]
                top_send[h] = b16(jnp.where(upper, comp[h][2], middle))
                top_copy(h).start()

    upper = ctx // (1 << (levels - 1)) == 1
    state, grad = {}, {}
    for h in range(heads):
        top_copy(h).wait_recv()
        got = top_recv[h]
        base = jnp.where(upper, got, b16(init_ref[h]))
        state[h] = dot_nn(b16(prefix[h][0]), base) + prefix[h][1]
        tail = jnp.where(upper, jnp.zeros_like(got), got)
        grad[h] = dot_tn(b16(suffix[h][0]), tail) + suffix[h][1]
        gi_send[h * width : (h + 1) * width] = b16(
            dot_tn(b16(own[h, 0]), b16(grad[h])) + own[h, 2]
        )

    def red_device(r):
        return {"dp": r // red_ctx, "ctx": lax.rem(r, red_ctx)}

    def piece(r):
        return pl.ds(pl.multiple_of(r * piece_rows, piece_rows), piece_rows)

    def not_me(r):
        return jnp.logical_or(r // red_ctx != dp, lax.rem(r, red_ctx) != ctx)

    def gi_copy(r):
        return pltpu.make_async_remote_copy(
            src_ref=gi_send.at[piece(r)], dst_ref=gi_recv.at[dp],
            send_sem=gi_ss.at[r], recv_sem=gi_rs,
            device_id=red_device(r), device_id_type=MESH,
        )

    def for_reds(body):
        def step(r, carry):
            @pl.when(not_me(r))
            def _():
                body(r)
            return carry

        lax.fori_loop(0, n_red, step, 0)

    def for_peers(body):
        def step(i, carry):
            body(lax.rem(me + i, n_src))
            return carry

        lax.fori_loop(1, n_src, step, 0)

    @pl.when(ctx == 0)
    def _():
        for_reds(lambda r: gi_copy(r).start())
        gi_recv[dp] = gi_send[piece(my_red)]

    def all_copy(src, dst, send_sem, recv_sem, peer):
        return pltpu.make_async_remote_copy(
            src_ref=src, dst_ref=dst.at[my_red],
            send_sem=send_sem.at[peer], recv_sem=recv_sem,
            device_id={"dp": peer // n_ctx, "ctx": lax.rem(peer, n_ctx)},
            device_id_type=MESH,
        )

    def drain(ref, sem):
        pltpu.make_async_copy(ref, ref, sem).wait()

    lane = lax.broadcasted_iota(jnp.int32, (MINI, width), 1)
    dl_rows = [jnp.zeros((MINI, width), F32) for _ in range(blocks)]

    def gradients(group):
        for b in range(blocks):
            for h in group:
                key = k_ref[rows(b), lanes(h)]
                val = v_ref[rows(b), lanes(h)].astype(F32)
                now = b16(state[h])
                run_x[h, b] = now
                res = dot_nn(key, now) - val
                run_res[h, b] = res
                step = b16(rate(b, h) * res)
                run_p[h, b] = step
                state[h] = state[h] - dot_tn(key, step)
                dq_ref[rows(b), lanes(h)] = b16(dot_nt(o_ref[rows(b), lanes(h)], b16(state[h])))
        for b in reversed(range(blocks)):
            for h in group:
                key = k_ref[rows(b), lanes(h)]
                total = grad[h] + qo[h, b]
                total16 = b16(total)
                kg = dot_nn(key, total16)
                drate = jnp.sum(kg * run_res[h, b], axis=1, keepdims=True)
                dlogit = -drate * slope[b * MINI : (b + 1) * MINI, h : h + 1]
                dl_rows[b] = jnp.where(lane == h, dlogit, dl_rows[b])
                rkg = rate(b, h) * kg
                rkg16 = b16(rkg)
                dv_ref[rows(b), lanes(h)] = rkg16
                grad[h] = total - dot_tn(key, rkg16)
                left = jnp.concatenate([run_p[h, b], rkg16], axis=1)
                right = jnp.concatenate([total16, run_x[h, b]], axis=1)
                dk_ref[rows(b), lanes(h)] = b16(-dot_nt(left, right))

    half = max(heads // 2, 1)
    gradients(list(range(half)))

    @pl.when(is_red)
    def _():
        @pl.when(ctx == 0)
        def _():
            drain(gi_recv.at[0 : n_dp - 1], gi_rs)

        @pl.when(ctx != 0)
        def _():
            drain(gi_recv.at[0:n_dp], gi_rs)

        gi_red[...] = b16(jnp.sum(gi_recv[...].astype(F32), axis=0))
        for_peers(lambda peer: all_copy(gi_red, gi_all, gi_as, gi_ar, peer).start())
        gi_all[my_red] = gi_red[...]

    gradients(list(range(half, heads)))

    dl_all = jnp.concatenate(dl_rows, axis=0)
    dl_t = jnp.transpose(dl_all)[:8]
    dl_send[...] = dl_t
    dl_copy.start()
    mine = jnp.concatenate(split(dl_t), axis=0)
    features = hid_ref.shape[1]
    gw_part[...] = jnp.zeros_like(gw_part)
    for r in range(features // SPAN):
        both = dot_nn(mine, hid_ref[:, r * SPAN : (r + 1) * SPAN])
        gw_part[r] = both[:8] + both[8:]

    def gw_copy(r):
        return pltpu.make_async_remote_copy(
            src_ref=gw_part.at[r], dst_ref=gw_recv.at[me],
            send_sem=gw_ss.at[r], recv_sem=gw_rs,
            device_id=red_device(r), device_id_type=MESH,
        )

    for_reds(lambda r: gw_copy(r).start())

    rw_copy.wait_recv()
    dl_copy.wait_recv()
    theirs = jnp.concatenate(split(dl_recv[...]), axis=0)
    for r in range(features // SPAN):
        cols = slice(r * SPAN, (r + 1) * SPAN)
        first = b16(dot_tn(mine, rw_ref[:, cols])).astype(F32)
        second = b16(dot_tn(theirs, rw_other[:, cols])).astype(F32)
        gh_ref[:, cols] = b16(first + second)

    @pl.when(is_red)
    def _():
        gw_recv[me] = gw_part[my_red]
        drain(gw_recv.at[0 : n_src - 1], gw_rs)
        gw_red[...] = jnp.sum(gw_recv[...], axis=0)
        for_peers(lambda peer: all_copy(gw_red, gw_all, gw_as, gw_ar, peer).start())
        gw_all[my_red] = gw_red[...]

    def finish(full, sem):
        @pl.when(is_red)
        def _():
            drain(full.at[0 : n_red - 1], sem)

        if n_ctx > red_ctx:
            @pl.when(jnp.logical_not(is_red))
            def _():
                drain(full.at[0:n_red], sem)

    finish(gi_all, gi_ar)
    gi_ref[...] = gi_all[...].astype(F32)
    finish(gw_all, gw_ar)
    gw_ref[...] = gw_all[...]

    for level in range(levels - 1):
        for h in range(heads):
            level_copy(level, h).wait_send()
    for h in range(heads):
        top_copy(h).wait_send()
    rw_copy.wait_send()
    dl_copy.wait_send()

    @pl.when(ctx == 0)
    def _():
        for_reds(lambda r: gi_copy(r).wait_send())

    for_reds(lambda r: gw_copy(r).wait_send())

    @pl.when(is_red)
    def _():
        for_peers(lambda peer: all_copy(gi_red, gi_all, gi_as, gi_ar, peer).wait_send())
        for_peers(lambda peer: all_copy(gw_red, gw_all, gw_as, gw_ar, peer).wait_send())


def local(n_dp, n_ctx, queries, keys, values, hidden_in, rate_weight, state_init, out_grad):
    seqs, toks, heads, width = queries.shape
    features = hidden_in.shape[2]
    n_red = n_dp * min(n_ctx, 4)
    n_src = n_dp * n_ctx
    levels = n_ctx.bit_length() - 1
    blocks = toks // MINI
    gap = jnp.zeros((8 - heads, features), BF16)
    weights = jnp.concatenate([rate_weight, gap, rate_weight, gap], axis=0)
    piece_rows = heads * width // n_red
    flat = (toks, heads * width)
    vmem = pl.BlockSpec(memory_space=pltpu.VMEM)
    dma = pltpu.SemaphoreType.DMA
    scratch = [
        pltpu.VMEM((heads, 3, width, width), F32),
        pltpu.VMEM((levels - 1, heads, 3, width, width), BF16),
        pltpu.VMEM((levels - 1, heads, 3, width, width), BF16),
        pltpu.VMEM((heads, width, width), BF16),
        pltpu.VMEM((heads, width, width), BF16),
        pltpu.VMEM((heads, blocks, width, width), F32),
        pltpu.VMEM((heads, blocks, width, width), BF16),
        pltpu.VMEM((heads, blocks, MINI, width), BF16),
        pltpu.VMEM((heads, blocks, MINI, width), F32),
        pltpu.VMEM((16, features), BF16),
        pltpu.VMEM((8, toks), F32),
        pltpu.VMEM((8, toks), F32),
        pltpu.VMEM((heads * width, width), BF16),
        pltpu.VMEM((n_dp, piece_rows, width), BF16),
        pltpu.VMEM((piece_rows, width), BF16),
        pltpu.VMEM((n_red, piece_rows, width), BF16),
        pltpu.VMEM((n_red, 8, SPAN), F32),
        pltpu.VMEM((n_src, 8, SPAN), F32),
        pltpu.VMEM((8, SPAN), F32),
        pltpu.VMEM((n_red, 8, SPAN), F32),
        dma((levels - 1, heads)), dma((levels - 1, heads)),
        dma((heads,)), dma((heads,)), dma((2,)), dma((2,)),
        dma((n_red,)), dma, dma((n_src,)), dma,
        dma((n_red,)), dma, dma((n_src,)), dma,
    ]
    dq, dk, dv, gh, gw, gi = pl.pallas_call(
        functools.partial(kernel, n_dp, n_ctx, n_red, heads, width, toks),
        out_shape=(
            jax.ShapeDtypeStruct(flat, BF16),
            jax.ShapeDtypeStruct(flat, BF16),
            jax.ShapeDtypeStruct(flat, BF16),
            jax.ShapeDtypeStruct((toks, features), BF16),
            jax.ShapeDtypeStruct((n_red, 8, SPAN), F32),
            jax.ShapeDtypeStruct((n_red, piece_rows, width), F32),
        ),
        in_specs=[vmem] * 7,
        out_specs=[vmem] * 6,
        scratch_shapes=scratch,
        compiler_params=pltpu.CompilerParams(
            collective_id=0, has_side_effects=True, vmem_limit_bytes=56 * 2**20
        ),
    )(
        queries.reshape(flat), keys.reshape(flat), values.reshape(flat),
        hidden_in.reshape(toks, features), weights, state_init, out_grad.reshape(flat),
    )
    grad_rate = jnp.transpose(gw, (1, 0, 2)).reshape(8, n_red * SPAN)[:heads, :features]
    shape = queries.shape
    return (
        dq.reshape(shape), dk.reshape(shape), dv.reshape(shape),
        gh.reshape(hidden_in.shape), grad_rate, gi.reshape(heads, width, width),
    )


def solution(mesh):
    placed = (
        P("dp", "ctx", "head", None),
        P("dp", "ctx", "head", None),
        P("dp", "ctx", "head", None),
        P("dp", "ctx", None),
        P("head", None),
        P("head", None, None),
        P("dp", "ctx", "head", None),
    )
    return jax.shard_map(
        functools.partial(local, mesh.shape["dp"], mesh.shape["ctx"]),
        mesh=mesh,
        in_specs=placed,
        out_specs=(
            P("dp", "ctx", "head", None),
            P("dp", "ctx", "head", None),
            P("dp", "ctx", "head", None),
            P("dp", "ctx", None),
            P("head", None),
            P("head", None, None),
        ),
        check_vma=False,
    )
```
